32 devices in a mesh: groups: 2 (over x), space: 16 (over z, y, core).
Axes of the slice: x: 2, y: 2, z: 4, core: 2. Of those that a mesh axis runs over, the one named last changes fastest.
Arguments:
- probes: float32 [8, 40, 32768], P('groups', None, 'space'), parts along dimension 0
- prior_std: float32 [65536], P(('groups', 'space')), parts along dimension 0, may hold values from 0.4 to 2
- blocks: bfloat16 [9216, 128, 128], P(('groups', 'space')), parts along dimension 0, may hold values from -0.5 to 0.5
- footprint_block_scale: float32 [9216], P(('groups', 'space')), parts along dimension 0, may hold values from 0.1 to 1
- block_lists: int32 [9216, 3], P(('groups', 'space')), parts along dimension 0, may hold values from 0 to 39, as said below
- block_live: int32 [32], P(('groups', 'space')), parts along dimension 0, may hold values from 1 to 288, as said below
- noise_inv: float32 [4096], P('groups'), parts along dimension 0, may hold values from 0.2 to 1
- corr_days: float32 [2], P('groups'), parts along dimension 0, may hold values from 3 to 12
Outputs:
- hess_probes: float32 [8, 40, 32768], P('groups', None, 'space'), parts along dimension 0
- curvature: float32 [8], P('groups'), parts along dimension 0
The draws below stay inside these ranges and needn't reach their ends.
There are 2 independent parts, one for each index of `groups`. The reference program is written for one: setup_inputs(seed, part) draws one part's arguments, and reference() takes and returns one part's arrays. A program takes and returns all parts, laid end to end along the dimension named above; each array names one. Nothing has to cross between parts.
Inputs may be any that keep to these rules, and one draw needn't show every extreme that they name: `block_lists`: column 0 lies in 0 to 15, column 1 in 0 to 15, column 2 in 0 to 39. `block_live`: some device has all 288 slots live in every draw.
All inputs are finite; a program needn't handle non-finite values.
Results may differ from the reference program's by a relative error of at most 0.0039.
Values may be sent and summed in bfloat16 or wider, within the bound.
A program may use at most 64 MiB of HBM per device.

```python
import math
import jax
import jax.numpy as jnp
from jax import lax

PROBES = 4
FLUX_DAY_COUNT = 40
TILES_PER_SHARD = 16
MAXB = 288
CELLS = 32768
RECEPTOR_BLOCKS = 16
RECEPTORS = 2048
SLOT_TOTAL = 4608
N_SPACE = 16


def draw_probes(key, part):
    key = jax.random.fold_in(key, 11)
    ramp = 1.0 + 0.75 * jnp.arange(CELLS).astype(jnp.float32) / CELLS
    base = jax.random.normal(key, (PROBES, FLUX_DAY_COUNT, CELLS), jnp.float32)
    return base * ramp[None, None, :]


def draw_block_lists(key, part):
    key = jax.random.fold_in(key, 23)
    first_term, second_term, third_term = jax.random.split(key, 3)
    receptor_block = jax.random.randint(first_term, (SLOT_TOTAL, 1), 0, RECEPTOR_BLOCKS)
    flux_tile = jax.random.randint(second_term, (SLOT_TOTAL, 1), 0, TILES_PER_SHARD)
    day_index = jax.random.randint(third_term, (SLOT_TOTAL, 1), 0, FLUX_DAY_COUNT)
    receptor_block = receptor_block.at[0, 0].set(RECEPTOR_BLOCKS - 1)
    day_index = day_index.at[1, 0].set(FLUX_DAY_COUNT - 1)
    return jnp.concatenate([receptor_block, flux_tile, day_index], axis=1).astype(jnp.int32)


def draw_block_live(key, part):
    key = jax.random.fold_in(key, 37)
    first_term, second_term = jax.random.split(key)
    counts = jax.random.randint(first_term, (N_SPACE,), max(MAXB // 3, 1), MAXB + 1)
    busiest = jax.random.randint(second_term, (), 0, N_SPACE)
    return jnp.where(jnp.arange(N_SPACE) == busiest, MAXB, counts).astype(jnp.int32)


def level_of(rng, extent, shards, smallest, high):
    factor_of, own = 1.0, jax.random.fold_in(rng, 6)
    for dim, parts in shards:
        draws = jnp.exp(jax.random.uniform(jax.random.fold_in(own, dim), (parts,), jnp.float32, smallest / len(shards), high / len(shards)))
        factor_of = factor_of * jnp.repeat(draws, extent[dim] // parts).reshape([-1 if axis == dim else 1 for axis in range(len(extent))])
    return factor_of


def scatter_about(own_key, extent, width, most, pieces=(), kind=jnp.bfloat16):
    entries = width * jax.random.normal(own_key, extent, jnp.float32)
    if pieces:
        entries = entries * level_of(own_key, extent, pieces, -0.22, 0.18)
    return jnp.clip(entries, -most, most).astype(kind)


def setup_inputs(seed: int = 0, part: int = 0) -> dict:
    arg_keys = jax.random.split(jax.random.key(seed), 9)
    own_keys = jax.random.split(jax.random.fold_in(arg_keys[8], part), 9)
    return {
        "probes": draw_probes(jax.random.fold_in(jax.random.fold_in(arg_keys[8], part), 71), part),
        "prior_std": jnp.clip(jnp.exp(math.log(2.0) - 1.609438 * jax.random.uniform(own_keys[1], (CELLS,), jnp.float32) ** level_of(own_keys[1], (CELLS,), ((0, 16),), -0.2, 0.2)), 0.4, 2.0),
        "blocks": scatter_about(own_keys[2], (SLOT_TOTAL, 128, 128), 128 ** -0.5, 0.5, ((0, 16),)),
        "footprint_block_scale": jnp.clip(jnp.exp(math.log(1.0) - 2.3025851 * jax.random.uniform(own_keys[3], (SLOT_TOTAL,), jnp.float32) ** level_of(own_keys[3], (SLOT_TOTAL,), ((0, 16),), -0.2, 0.2)), 0.1, 1.0),
        "block_lists": draw_block_lists(jax.random.fold_in(jax.random.fold_in(arg_keys[8], part), 71), part),
        "block_live": draw_block_live(jax.random.fold_in(jax.random.fold_in(arg_keys[8], part), 71), part),
        "noise_inv": jnp.clip(jnp.exp(jax.random.uniform(own_keys[6], (RECEPTORS,), jnp.float32, math.log(0.2), math.log(1.0))), 0.2, 1.0),
        "corr_days": jnp.clip(jnp.exp(jax.random.uniform(own_keys[7], (1,), jnp.float32, math.log(3.0), math.log(12.0))), 3.0, 12.0),
    }


def temporal_factor(corr_days, days):
    index = jnp.arange(days).astype(jnp.float32)
    corr = jnp.exp(-jnp.abs(index[:, None] - index[None, :]) / corr_days[0])
    return jnp.linalg.cholesky(corr)

def reference(probes, prior_std, blocks, footprint_block_scale, block_lists, block_live, noise_inv, corr_days):
    factor = temporal_factor(corr_days, FLUX_DAY_COUNT)
    moved = jnp.einsum('ts,psc->ptc', factor, probes, precision=lax.Precision.HIGHEST)
    scaled = (moved * prior_std[None, None, :]).astype(jnp.bfloat16)
    grid = scaled.reshape(PROBES, FLUX_DAY_COUNT, N_SPACE, TILES_PER_SHARD, 128).transpose(2, 0, 1, 3, 4)
    grid = grid.reshape(N_SPACE, PROBES, FLUX_DAY_COUNT * TILES_PER_SHARD, 128)
    dev_blocks = blocks.reshape(N_SPACE, MAXB, 128, 128)
    dev_lists = block_lists.reshape(N_SPACE, MAXB, 3)
    live = (jnp.arange(MAXB)[None, :] < block_live[:, None]).astype(jnp.float32)
    dev_weight = footprint_block_scale.reshape(N_SPACE, MAXB) * live
    keys = dev_lists[:, :, 2] * TILES_PER_SHARD + dev_lists[:, :, 1]

    def forward(total, items):
        dev_grid, blk, lists, weight, key = items
        picked = jnp.take(dev_grid, key, axis=1).astype(jnp.float32)
        part = jnp.einsum('pbc,brc->bpr', picked, blk.astype(jnp.float32)) * weight[:, None, None]
        return (total + jax.ops.segment_sum(part, lists[:, 0], num_segments=RECEPTOR_BLOCKS), 0)
    obs, _ = lax.scan(forward, jnp.zeros((RECEPTOR_BLOCKS, PROBES, 128), jnp.float32), (grid, dev_blocks, dev_lists, dev_weight, keys))
    resid = (obs * noise_inv.reshape(RECEPTOR_BLOCKS, 1, 128)).astype(jnp.bfloat16)

    def backward(items):
        blk, lists, weight, key = items
        picked = jnp.take(resid, lists[:, 0], axis=0).astype(jnp.float32)
        part = jnp.einsum('bpr,brc->bpc', picked, blk.astype(jnp.float32)) * weight[:, None, None]
        return jax.ops.segment_sum(part, key, num_segments=FLUX_DAY_COUNT * TILES_PER_SHARD)
    grads = lax.map(backward, (dev_blocks, dev_lists, dev_weight, keys))
    grads = grads.reshape(N_SPACE, FLUX_DAY_COUNT, TILES_PER_SHARD, PROBES, 128).transpose(3, 1, 0, 2, 4)
    back = grads.reshape(PROBES, FLUX_DAY_COUNT, CELLS) * prior_std[None, None, :]
    hess_probes = probes + jnp.einsum('ts,ptc->psc', factor, back, precision=lax.Precision.HIGHEST)
    curvature = jnp.sum(probes * hess_probes, axis=(1, 2))
    return (hess_probes, curvature)
```

```python
import functools

import jax
import jax.numpy as jnp
from jax import lax
from jax.experimental import pallas as pl
from jax.experimental.pallas import tpu as pltpu
from jax.sharding import PartitionSpec as P

MESH = pl.DeviceIdType.MESH
CHUNKS = 8
PAD = 8


def split(x):
    high = x.astype(jnp.bfloat16)
    return high, (x - high.astype(jnp.float32)).astype(jnp.bfloat16)


def mm(a, b):
    return jnp.dot(a, b, preferred_element_type=jnp.float32)


def kernel(
    n,
    lists_s,
    live_s,
    corr_ref,
    lists_v,
    scale_ref,
    prior_ref,
    noise_ref,
    probes_hbm,
    blocks_hbm,
    hess_ref,
    curv_ref,
    x_buf,
    b_buf,
    s_buf,
    parts,
    res_buf,
    spread,
    snd,
    rc1,
    gat,
    x_sem,
    b_sem,
    send1,
    recv1,
    send2,
    recv2,
):
    rows, cells = x_buf.shape
    count = 4
    days = rows // count
    tiles = cells // 128
    slots = lists_v.shape[1]
    rec = noise_ref.shape[0]
    own = rec // n
    per = slots // CHUNKS
    f32 = jnp.float32
    me = lax.axis_index("space")

    x_copy = pltpu.make_async_copy(probes_hbm, x_buf, x_sem)
    x_copy.start()
    b_copies = []
    for c in range(CHUNKS):
        part = pl.ds(c * per * 128, per * 128)
        cp = pltpu.make_async_copy(blocks_hbm.at[part], b_buf.at[part], b_sem.at[c])
        cp.start()
        b_copies.append(cp)

    barrier = pltpu.get_barrier_semaphore()

    @pl.loop(1, n)
    def _(o):
        pl.semaphore_signal(
            barrier, inc=1, device_id={"space": lax.rem(me + o, n)}, device_id_type=MESH
        )

    rate = -1.0 / corr_ref[...]
    rest = jnp.sqrt(1.0 - jnp.exp(2.0 * rate))

    row = lax.broadcasted_iota(jnp.int32, (rows, 1), 0)
    col = lax.broadcasted_iota(jnp.int32, (1, rows), 1)
    row_t, row_p = row // count, row % count
    col_p = sum((col >= days * p).astype(jnp.int32) for p in range(1, count))
    col_s = col - days * col_p
    lag = row_t - col_s
    value = jnp.exp(rate * lag.astype(f32)) * jnp.where(col_s == 0, 1.0, rest)
    factor = jnp.where((lag >= 0) & (row_p == col_p), value, 0.0)
    f_hi, f_lo = split(factor)

    r_k, j_k, t_k = lists_v[0:1, :], lists_v[1:2, :], lists_v[2:3, :]
    lane = lax.broadcasted_iota(jnp.int32, (1, slots), 1)
    weight = jnp.where(lane < live_s[0], scale_ref[...], 0.0)

    s_buf[0:PAD, :] = jnp.zeros((PAD, 128), f32)
    s_buf[PAD + tiles * rows :, :] = jnp.zeros((PAD, 128), f32)
    res_buf[0:PAD, :] = jnp.zeros((PAD, 128), f32)
    res_buf[PAD + rec * count :, :] = jnp.zeros((PAD, 128), f32)

    x_copy.wait()
    square = jnp.zeros((rows, 128), f32)
    for j in range(0, tiles, 2):
        x = x_buf[:, j * 128 : j * 128 + 256]
        square = square + x[:, :128] * x[:, :128] + x[:, 128:] * x[:, 128:]
        x_hi, x_lo = split(x)
        moved = mm(f_hi, x_hi) + mm(f_hi, x_lo) + mm(f_lo, x_hi)
        scaled = (moved * prior_ref[:, j * 128 : j * 128 + 256]).astype(jnp.bfloat16).astype(f32)
        s_buf[PAD + j * rows : PAD + (j + 1) * rows, :] = scaled[:, :128]
        s_buf[PAD + (j + 1) * rows : PAD + (j + 2) * rows, :] = scaled[:, 128:]
    norm = jnp.sum(square.reshape(count, days, 128), axis=1)
    norm = jnp.concatenate([jnp.zeros_like(norm), norm], axis=0)

    low = lax.broadcasted_iota(jnp.int32, (8, 128), 0) < 4

    def forward(q, carry):
        k = q * 4

        def at(i):
            return PAD + lists_s[1, k + i] * rows + lists_s[2, k + i] * count

        a = jnp.where(low, s_buf[pl.ds(at(0), 8), :], s_buf[pl.ds(at(1) - 4, 8), :])
        b = jnp.where(low, s_buf[pl.ds(at(2), 8), :], s_buf[pl.ds(at(3) - 4, 8), :])
        lhs = jnp.concatenate([a, b], axis=0).astype(jnp.bfloat16)
        rhs = b_buf[pl.ds(pl.multiple_of(q * 512, 512), 512), :]
        o = lax.dot_general(lhs, rhs, (((1,), (1,)), ((), ())), preferred_element_type=f32)
        top = jnp.where(low, o[0:8, 0:128], o[0:8, 128:256])
        bot = jnp.where(low, o[8:16, 256:384], o[8:16, 384:512])
        parts[pl.ds(pl.multiple_of(q * 16, 16), 16), :] = jnp.concatenate([top, bot], axis=0)
        return carry

    quads = per // 4
    for c in range(CHUNKS):
        b_copies[c].wait()
        lax.fori_loop(c * quads, (c + 1) * quads, forward, 0, unroll=3)

    srow = lax.broadcasted_iota(jnp.int32, (rec * 8, 1), 0)
    pick = jnp.where(srow // 8 == r_k, weight, 0.0)
    obs = jnp.zeros((rec * 8, 128), f32)
    for p in range(count):
        h_hi, h_lo = split(jnp.where(srow % 8 == p, pick, 0.0))
        v_hi, v_lo = split(parts[pl.ds(p, slots, stride=count), :])
        obs = obs + mm(h_hi, v_hi) + mm(h_hi, v_lo) + mm(h_lo, v_hi)
    snd[...] = (obs.reshape(rec, 8, 128) + norm[None]).reshape(n, own, 8, 128)

    pl.semaphore_wait(barrier, n - 1)

    def first(o):
        peer = lax.rem(me + o, n)
        return pltpu.make_async_remote_copy(
            src_ref=snd.at[peer],
            dst_ref=rc1.at[me],
            send_sem=send1.at[peer],
            recv_sem=recv1.at[me],
            device_id={"space": peer},
            device_id_type=MESH,
        )

    def second(o):
        peer = lax.rem(me + o, n)
        return pltpu.make_async_remote_copy(
            src_ref=gat.at[me],
            dst_ref=gat.at[me],
            send_sem=send2.at[peer],
            recv_sem=recv2.at[me],
            device_id={"space": peer},
            device_id_type=MESH,
        )

    def arrived(buf, sem, o):
        peer = lax.rem(me + o, n)
        return pltpu.make_async_remote_copy(
            src_ref=buf.at[peer],
            dst_ref=buf.at[peer],
            send_sem=sem.at[peer],
            recv_sem=sem.at[peer],
            device_id={"space": peer},
            device_id_type=MESH,
        )

    @pl.loop(1, n)
    def _(o):
        first(o).start()

    rc1[me] = snd[me]

    day = lax.broadcasted_iota(jnp.int32, (days, 1), 0)
    late = t_k - day
    grow = jnp.exp(rate * late.astype(f32)) * jnp.where(day == 0, 1.0, rest)
    grow = jnp.where(late >= 0, grow, 0.0) * weight
    for j in range(tiles):
        spread[j * days : (j + 1) * days, :] = jnp.where(j_k == j, grow, 0.0)

    @pl.loop(1, n)
    def _(o):
        arrived(rc1, recv1, o).wait_recv()

    gat[me] = jnp.sum(rc1[...], axis=0)

    @pl.loop(1, n)
    def _(o):
        second(o).start()

    @pl.loop(1, n)
    def _(o):
        first(o).wait_send()

    @pl.loop(1, n)
    def _(o):
        arrived(gat, recv2, o).wait_recv()

    total = gat[...].reshape(rec, 8, 128)
    resid = (total * noise_ref[...][:, None, :]).astype(jnp.bfloat16).astype(f32)
    for r in range(rec):
        res_buf[PAD + r * count : PAD + (r + 1) * count, :] = resid[r, :count, :]
    energy = jnp.sum(total * resid, axis=0)
    energy = energy[:count] + total[0, count:]
    curv_ref[...] = jnp.broadcast_to(jnp.sum(energy, axis=1, keepdims=True), (count, 128))

    def backward(q, carry):
        k = q * 4

        def at(i):
            return PAD + lists_s[0, k + i] * count

        outs = []
        for h in range(2):
            a = jnp.where(low, res_buf[pl.ds(at(2 * h), 8), :], 0.0)
            b = jnp.where(low, 0.0, res_buf[pl.ds(at(2 * h + 1) - 4, 8), :])
            lhs = jnp.concatenate([a, b], axis=1).astype(jnp.bfloat16)
            rhs = b_buf[pl.ds(pl.multiple_of(q * 512 + h * 256, 256), 256), :]
            outs.append(mm(lhs, rhs))
        parts[pl.ds(pl.multiple_of(q * 16, 16), 16), :] = jnp.concatenate(outs, axis=0)
        return carry

    lax.fori_loop(0, slots // 4, backward, 0, unroll=4)

    g_hi = spread[...].astype(jnp.bfloat16)
    for p in range(count):
        v_hi = parts[pl.ds(p, slots, stride=count), :].astype(jnp.bfloat16)
        image = mm(g_hi, v_hi)
        for j in range(tiles):
            here = (slice(p * days, (p + 1) * days), slice(j * 128, (j + 1) * 128))
            back = image[j * days : (j + 1) * days, :] * prior_ref[:, j * 128 : (j + 1) * 128]
            hess_ref[here] = x_buf[here] + back

    @pl.loop(1, n)
    def _(o):
        second(o).wait_send()


def shards(
    n, probes, prior_std, blocks, footprint_block_scale, block_lists, block_live, noise_inv, corr_days
):
    count, days, cells = probes.shape
    slots = blocks.shape[0]
    rec = noise_inv.shape[0] // 128
    rows = count * days
    tiles = cells // 128
    own = rec // n
    lists = block_lists.T
    vmem = pl.BlockSpec(memory_space=pltpu.VMEM)
    smem = pl.BlockSpec(memory_space=pltpu.SMEM)
    hbm = pl.BlockSpec(memory_space=pl.ANY)
    dma = pltpu.SemaphoreType.DMA
    hess, curv = pl.pallas_call(
        functools.partial(kernel, n),
        out_shape=(
            jax.ShapeDtypeStruct((rows, cells), jnp.float32),
            jax.ShapeDtypeStruct((count, 128), jnp.float32),
        ),
        in_specs=[smem, smem, vmem, vmem, vmem, vmem, vmem, hbm, hbm],
        out_specs=(vmem, vmem),
        scratch_shapes=[
            pltpu.VMEM((rows, cells), jnp.float32),
            pltpu.VMEM((slots * 128, 128), jnp.bfloat16),
            pltpu.VMEM((tiles * rows + 2 * PAD, 128), jnp.float32),
            pltpu.VMEM((slots * count, 128), jnp.float32),
            pltpu.VMEM((rec * count + 2 * PAD, 128), jnp.float32),
            pltpu.VMEM((tiles * days, slots), jnp.float32),
            pltpu.VMEM((n, own, 8, 128), jnp.float32),
            pltpu.VMEM((n, own, 8, 128), jnp.float32),
            pltpu.VMEM((n, own, 8, 128), jnp.float32),
            dma(()),
            dma((CHUNKS,)),
            dma((n,)),
            dma((n,)),
            dma((n,)),
            dma((n,)),
        ],
        compiler_params=pltpu.CompilerParams(
            collective_id=0, has_side_effects=True, vmem_limit_bytes=48 * 1024 * 1024
        ),
    )(
        lists,
        block_live,
        corr_days.reshape(1, 1),
        lists,
        footprint_block_scale.reshape(1, slots),
        prior_std.reshape(1, cells),
        noise_inv.reshape(rec, 128),
        probes.reshape(rows, cells),
        blocks.reshape(slots * 128, 128),
    )
    return hess.reshape(count, days, cells), curv[:, 0]


def solution(mesh):
    in_specs = (
        P("groups", None, "space"),
        P(("groups", "space")),
        P(("groups", "space"), None, None),
        P(("groups", "space")),
        P(("groups", "space"), None),
        P(("groups", "space")),
        P("groups"),
        P("groups"),
    )
    out_specs = (P("groups", None, "space"), P("groups"))
    return jax.shard_map(
        functools.partial(shards, mesh.shape["space"]),
        mesh=mesh,
        in_specs=in_specs,
        out_specs=out_specs,
        check_vma=False,
    )
```

```python
import functools

import jax
import jax.numpy as jnp
from jax import lax
from jax.experimental import pallas as pl
from jax.experimental.pallas import tpu as pltpu
from jax.sharding import PartitionSpec as P

MESH = pl.DeviceIdType.MESH
CHUNKS = 8
PAD = 8
LIMIT = 48 * 1024 * 1024


def hold(x):
    return pltpu.with_memory_space_constraint(x, pltpu.HBM)


def split(x):
    high = x.astype(jnp.bfloat16)
    return high, (x - high.astype(jnp.float32)).astype(jnp.bfloat16)


def mm(a, b):
    return jnp.dot(a, b, preferred_element_type=jnp.float32)


def kernel(
    n,
    live_s,
    corr_s,
    lists_hbm,
    scale_hbm,
    prior_hbm,
    noise_hbm,
    probes_hbm,
    blocks_hbm,
    hess_ref,
    curv_ref,
    lists_s,
    lists_v,
    scale_ref,
    prior_ref,
    noise_ref,
    x_buf,
    b_buf,
    s_buf,
    parts,
    res_buf,
    spread,
    snd,
    rc1,
    gat,
    in_sem,
    b_sem,
    send1,
    recv1,
    send2,
    recv2,
):
    rows, cells = x_buf.shape
    count = 4
    days = rows // count
    tiles = cells // 128
    slots = lists_v.shape[1]
    rec = noise_ref.shape[0]
    own = rec // n
    per = slots // CHUNKS
    f32 = jnp.float32
    me = lax.axis_index("space")

    x_copy = pltpu.make_async_copy(probes_hbm, x_buf, in_sem.at[0])
    x_copy.start()
    small = []
    for i, (src, dst) in enumerate(
        (
            (lists_hbm, lists_s),
            (lists_hbm, lists_v),
            (scale_hbm, scale_ref),
            (prior_hbm, prior_ref),
            (noise_hbm, noise_ref),
        )
    ):
        cp = pltpu.make_async_copy(src, dst, in_sem.at[i + 1])
        cp.start()
        small.append(cp)
    b_copies = []
    for c in range(CHUNKS):
        part = pl.ds(c * per * 128, per * 128)
        cp = pltpu.make_async_copy(blocks_hbm.at[part], b_buf.at[part], b_sem.at[c])
        cp.start()
        b_copies.append(cp)

    barrier = pltpu.get_barrier_semaphore()

    @pl.loop(1, n)
    def _(o):
        pl.semaphore_signal(
            barrier, inc=1, device_id={"space": lax.rem(me + o, n)}, device_id_type=MESH
        )

    rate = -1.0 / jnp.full((1, 1), corr_s[0], f32)
    rest = jnp.sqrt(1.0 - jnp.exp(2.0 * rate))

    row = lax.broadcasted_iota(jnp.int32, (rows, 1), 0)
    col = lax.broadcasted_iota(jnp.int32, (1, rows), 1)
    row_t, row_p = row // count, row % count
    col_p = sum((col >= days * p).astype(jnp.int32) for p in range(1, count))
    col_s = col - days * col_p
    lag = row_t - col_s
    value = jnp.exp(rate * lag.astype(f32)) * jnp.where(col_s == 0, 1.0, rest)
    factor = jnp.where((lag >= 0) & (row_p == col_p), value, 0.0)
    f_hi, f_lo = split(factor)

    for cp in small:
        cp.wait()

    r_k, j_k, t_k = lists_v[0:1, :], lists_v[1:2, :], lists_v[2:3, :]
    lane = lax.broadcasted_iota(jnp.int32, (1, slots), 1)
    weight = jnp.where(lane < live_s[0], scale_ref[...].reshape(1, slots), 0.0)

    s_buf[0:PAD, :] = jnp.zeros((PAD, 128), f32)
    s_buf[PAD + tiles * rows :, :] = jnp.zeros((PAD, 128), f32)
    res_buf[0:PAD, :] = jnp.zeros((PAD, 128), f32)
    res_buf[PAD + rec * count :, :] = jnp.zeros((PAD, 128), f32)

    x_copy.wait()
    square = jnp.zeros((rows, 128), f32)
    for j in range(0, tiles, 2):
        x = x_buf[:, j * 128 : j * 128 + 256]
        square = square + x[:, :128] * x[:, :128] + x[:, 128:] * x[:, 128:]
        x_hi, x_lo = split(x)
        moved = mm(f_hi, x_hi) + mm(f_hi, x_lo) + mm(f_lo, x_hi)
        scaled = (moved * prior_ref[:, j * 128 : j * 128 + 256]).astype(jnp.bfloat16).astype(f32)
        s_buf[PAD + j * rows : PAD + (j + 1) * rows, :] = scaled[:, :128]
        s_buf[PAD + (j + 1) * rows : PAD + (j + 2) * rows, :] = scaled[:, 128:]
    norm = jnp.sum(square.reshape(count, days, 128), axis=1)
    norm = jnp.concatenate([jnp.zeros_like(norm), norm], axis=0)

    low = lax.broadcasted_iota(jnp.int32, (8, 128), 0) < 4

    def forward(q, carry):
        k = q * 4

        def at(i):
            return PAD + lists_s[1, k + i] * rows + lists_s[2, k + i] * count

        a = jnp.where(low, s_buf[pl.ds(at(0), 8), :], s_buf[pl.ds(at(1) - 4, 8), :])
        b = jnp.where(low, s_buf[pl.ds(at(2), 8), :], s_buf[pl.ds(at(3) - 4, 8), :])
        lhs = jnp.concatenate([a, b], axis=0).astype(jnp.bfloat16)
        rhs = b_buf[pl.ds(pl.multiple_of(q * 512, 512), 512), :]
        o = lax.dot_general(lhs, rhs, (((1,), (1,)), ((), ())), preferred_element_type=f32)
        top = jnp.where(low, o[0:8, 0:128], o[0:8, 128:256])
        bot = jnp.where(low, o[8:16, 256:384], o[8:16, 384:512])
        parts[pl.ds(pl.multiple_of(q * 16, 16), 16), :] = jnp.concatenate([top, bot], axis=0)
        return carry

    quads = per // 4
    for c in range(CHUNKS):
        b_copies[c].wait()
        lax.fori_loop(c * quads, (c + 1) * quads, forward, 0, unroll=9)

    srow = lax.broadcasted_iota(jnp.int32, (rec * 8, 1), 0)
    pick = jnp.where(srow // 8 == r_k, weight, 0.0)
    obs = jnp.zeros((rec * 8, 128), f32)
    for p in range(count):
        h_hi, h_lo = split(jnp.where(srow % 8 == p, pick, 0.0))
        v_hi, v_lo = split(parts[pl.ds(p, slots, stride=count), :])
        obs = obs + mm(h_hi, v_hi) + mm(h_hi, v_lo) + mm(h_lo, v_hi)
    snd[...] = (obs.reshape(rec, 8, 128) + norm[None]).reshape(n, own, 8, 128)

    pl.semaphore_wait(barrier, n - 1)

    def first(o):
        peer = lax.rem(me + o, n)
        return pltpu.make_async_remote_copy(
            src_ref=snd.at[peer],
            dst_ref=rc1.at[me],
            send_sem=send1.at[peer],
            recv_sem=recv1.at[me],
            device_id={"space": peer},
            device_id_type=MESH,
        )

    def second(o):
        peer = lax.rem(me + o, n)
        return pltpu.make_async_remote_copy(
            src_ref=gat.at[me],
            dst_ref=gat.at[me],
            send_sem=send2.at[peer],
            recv_sem=recv2.at[me],
            device_id={"space": peer},
            device_id_type=MESH,
        )

    def arrived(buf, sem, o):
        peer = lax.rem(me + o, n)
        return pltpu.make_async_remote_copy(
            src_ref=buf.at[peer],
            dst_ref=buf.at[peer],
            send_sem=sem.at[peer],
            recv_sem=sem.at[peer],
            device_id={"space": peer},
            device_id_type=MESH,
        )

    @pl.loop(1, n)
    def _(o):
        first(o).start()

    rc1[me] = snd[me]

    day = lax.broadcasted_iota(jnp.int32, (days, 1), 0)
    late = t_k - day
    grow = jnp.exp(rate * late.astype(f32)) * jnp.where(day == 0, 1.0, rest)
    grow = jnp.where(late >= 0, grow, 0.0) * weight
    for j in range(tiles):
        spread[j * days : (j + 1) * days, :] = jnp.where(j_k == j, grow, 0.0)

    @pl.loop(1, n)
    def _(o):
        arrived(rc1, recv1, o).wait_recv()

    gat[me] = jnp.sum(rc1[...], axis=0)

    @pl.loop(1, n)
    def _(o):
        second(o).start()

    @pl.loop(1, n)
    def _(o):
        first(o).wait_send()

    @pl.loop(1, n)
    def _(o):
        arrived(gat, recv2, o).wait_recv()

    total = gat[...].reshape(rec, 8, 128)
    resid = (total * noise_ref[...][:, None, :]).astype(jnp.bfloat16).astype(f32)
    for r in range(rec):
        res_buf[PAD + r * count : PAD + (r + 1) * count, :] = resid[r, :count, :]
    energy = jnp.sum(total * resid, axis=0)
    energy = energy[:count] + total[0, count:]
    curv_ref[...] = jnp.broadcast_to(jnp.sum(energy, axis=1, keepdims=True), (count, 128))

    def backward(q, carry):
        k = q * 4

        def at(i):
            return PAD + lists_s[0, k + i] * count

        outs = []
        for h in range(2):
            a = jnp.where(low, res_buf[pl.ds(at(2 * h), 8), :], 0.0)
            b = jnp.where(low, 0.0, res_buf[pl.ds(at(2 * h + 1) - 4, 8), :])
            lhs = jnp.concatenate([a, b], axis=1).astype(jnp.bfloat16)
            rhs = b_buf[pl.ds(pl.multiple_of(q * 512 + h * 256, 256), 256), :]
            outs.append(mm(lhs, rhs))
        parts[pl.ds(pl.multiple_of(q * 16, 16), 16), :] = jnp.concatenate(outs, axis=0)
        return carry

    lax.fori_loop(0, slots // 4, backward, 0, unroll=12)

    g_hi = spread[...].astype(jnp.bfloat16)
    for p in range(count):
        v_hi = parts[pl.ds(p, slots, stride=count), :].astype(jnp.bfloat16)
        image = mm(g_hi, v_hi)
        for j in range(tiles):
            here = (slice(p * days, (p + 1) * days), slice(j * 128, (j + 1) * 128))
            back = image[j * days : (j + 1) * days, :] * prior_ref[:, j * 128 : (j + 1) * 128]
            hess_ref[here] = x_buf[here] + back

    @pl.loop(1, n)
    def _(o):
        second(o).wait_send()


def shards(
    n, probes, prior_std, blocks, footprint_block_scale, block_lists, block_live, noise_inv, corr_days
):
    count, days, cells = probes.shape
    slots = blocks.shape[0]
    rec = noise_inv.shape[0] // 128
    rows = count * days
    tiles = cells // 128
    own = rec // n
    vmem = pl.BlockSpec(memory_space=pltpu.VMEM)
    smem = pl.BlockSpec(memory_space=pltpu.SMEM)
    hbm = pl.BlockSpec(memory_space=pltpu.HBM)
    dma = pltpu.SemaphoreType.DMA
    hess, curv = pl.pallas_call(
        functools.partial(kernel, n),
        out_shape=(
            jax.ShapeDtypeStruct((rows, cells), jnp.float32),
            jax.ShapeDtypeStruct((count, 128), jnp.float32),
        ),
        in_specs=[smem, smem] + [hbm] * 6,
        out_specs=(vmem, vmem),
        scratch_shapes=[
            pltpu.SMEM((3, slots), jnp.int32),
            pltpu.VMEM((3, slots), jnp.int32),
            pltpu.VMEM((slots,), jnp.float32),
            pltpu.VMEM((1, cells), jnp.float32),
            pltpu.VMEM((rec, 128), jnp.float32),
            pltpu.VMEM((rows, cells), jnp.float32),
            pltpu.VMEM((slots * 128, 128), jnp.bfloat16),
            pltpu.VMEM((tiles * rows + 2 * PAD, 128), jnp.float32),
            pltpu.VMEM((slots * count, 128), jnp.float32),
            pltpu.VMEM((rec * count + 2 * PAD, 128), jnp.float32),
            pltpu.VMEM((tiles * days, slots), jnp.float32),
            pltpu.VMEM((n, own, 8, 128), jnp.float32),
            pltpu.VMEM((n, own, 8, 128), jnp.float32),
            pltpu.VMEM((n, own, 8, 128), jnp.float32),
            dma((6,)),
            dma((CHUNKS,)),
            dma((n,)),
            dma((n,)),
            dma((n,)),
            dma((n,)),
        ],
        compiler_params=pltpu.CompilerParams(
            collective_id=0, has_side_effects=True, vmem_limit_bytes=LIMIT
        ),
    )(
        block_live,
        corr_days,
        hold(block_lists.T),
        hold(footprint_block_scale),
        hold(prior_std.reshape(1, cells)),
        hold(noise_inv.reshape(rec, 128)),
        hold(probes.reshape(rows, cells)),
        blocks.reshape(slots * 128, 128),
    )
    return hess.reshape(count, days, cells), curv[:, 0]


def solution(mesh):
    in_specs = (
        P("groups", None, "space"),
        P(("groups", "space")),
        P(("groups", "space"), None, None),
        P(("groups", "space")),
        P(("groups", "space"), None),
        P(("groups", "space")),
        P("groups"),
        P("groups"),
    )
    out_specs = (P("groups", None, "space"), P("groups"))
    return jax.shard_map(
        functools.partial(shards, mesh.shape["space"]),
        mesh=mesh,
        in_specs=in_specs,
        out_specs=out_specs,
        check_vma=False,
    )
```

```python
import functools

import jax
import jax.numpy as jnp
from jax import lax
from jax.experimental import pallas as pl
from jax.experimental.pallas import tpu as pltpu
from jax.sharding import PartitionSpec as P

MESH = pl.DeviceIdType.MESH
CHUNKS = 3
PAD = 8
LIMIT = 48 * 1024 * 1024


def hold(x):
    return pltpu.with_memory_space_constraint(x, pltpu.HBM)


def split(x):
    high = x.astype(jnp.bfloat16)
    return high, (x - high.astype(jnp.float32)).astype(jnp.bfloat16)


def mm(a, b):
    return jnp.dot(a, b, preferred_element_type=jnp.float32)


def kernel(
    n,
    live_s,
    corr_s,
    lists_hbm,
    scale_hbm,
    prior_hbm,
    noise_hbm,
    probes_hbm,
    blocks_hbm,
    hess_ref,
    curv_ref,
    lists_s,
    lists_v,
    scale_ref,
    prior_ref,
    noise_ref,
    x_buf,
    b_buf,
    s_buf,
    parts,
    res_buf,
    spread,
    snd,
    rc1,
    gat,
    in_sem,
    b_sem,
    send1,
    recv1,
    send2,
    recv2,
):
    rows, cells = x_buf.shape
    count = 4
    days = rows // count
    tiles = cells // 128
    slots = lists_v.shape[1]
    rec = noise_ref.shape[0]
    own = rec // n
    per = slots // CHUNKS
    f32 = jnp.float32
    me = lax.axis_index("space")

    x_copy = pltpu.make_async_copy(probes_hbm, x_buf, in_sem.at[0])
    x_copy.start()
    small = []
    for i, (src, dst) in enumerate(
        (
            (lists_hbm, lists_s),
            (lists_hbm, lists_v),
            (scale_hbm, scale_ref),
            (prior_hbm, prior_ref),
            (noise_hbm, noise_ref),
        )
    ):
        cp = pltpu.make_async_copy(src, dst, in_sem.at[i + 1])
        cp.start()
        small.append(cp)
    b_copies = []
    for c in range(CHUNKS):
        part = pl.ds(c * per * 128, per * 128)
        cp = pltpu.make_async_copy(blocks_hbm.at[part], b_buf.at[part], b_sem.at[c])
        cp.start()
        b_copies.append(cp)

    barrier = pltpu.get_barrier_semaphore()

    @pl.loop(1, n)
    def _(o):
        pl.semaphore_signal(
            barrier, inc=1, device_id={"space": lax.rem(me + o, n)}, device_id_type=MESH
        )

    rate = -1.0 / jnp.full((1, 1), corr_s[0], f32)
    rest = jnp.sqrt(1.0 - jnp.exp(2.0 * rate))

    row = lax.broadcasted_iota(jnp.int32, (rows, 1), 0)
    col = lax.broadcasted_iota(jnp.int32, (1, rows), 1)
    row_t, row_p = row // count, row % count
    col_p = sum((col >= days * p).astype(jnp.int32) for p in range(1, count))
    col_s = col - days * col_p
    lag = row_t - col_s
    value = jnp.exp(rate * lag.astype(f32)) * jnp.where(col_s == 0, 1.0, rest)
    factor = jnp.where((lag >= 0) & (row_p == col_p), value, 0.0)
    f_hi, f_lo = split(factor)

    for cp in small:
        cp.wait()

    r_k, j_k, t_k = lists_v[0:1, :], lists_v[1:2, :], lists_v[2:3, :]
    lane = lax.broadcasted_iota(jnp.int32, (1, slots), 1)
    weight = jnp.where(lane < live_s[0], scale_ref[...].reshape(1, slots), 0.0)

    s_buf[0:PAD, :] = jnp.zeros((PAD, 128), f32)
    s_buf[PAD + tiles * rows :, :] = jnp.zeros((PAD, 128), f32)
    res_buf[0:PAD, :] = jnp.zeros((PAD, 128), f32)
    res_buf[PAD + rec * count :, :] = jnp.zeros((PAD, 128), f32)

    x_copy.wait()
    square = jnp.zeros((rows, 128), f32)
    for j in range(0, tiles, 2):
        x = x_buf[:, j * 128 : j * 128 + 256]
        square = square + x[:, :128] * x[:, :128] + x[:, 128:] * x[:, 128:]
        x_hi, x_lo = split(x)
        moved = mm(f_hi, x_hi) + mm(f_hi, x_lo) + mm(f_lo, x_hi)
        scaled = (moved * prior_ref[:, j * 128 : j * 128 + 256]).astype(jnp.bfloat16).astype(f32)
        s_buf[PAD + j * rows : PAD + (j + 1) * rows, :] = scaled[:, :128]
        s_buf[PAD + (j + 1) * rows : PAD + (j + 2) * rows, :] = scaled[:, 128:]
    norm = jnp.sum(square.reshape(count, days, 128), axis=1)
    norm = jnp.concatenate([jnp.zeros_like(norm), norm], axis=0)

    low = lax.broadcasted_iota(jnp.int32, (8, 128), 0) < 4

    def forward(q, carry):
        k = q * 4

        def at(i):
            return PAD + lists_s[1, k + i] * rows + lists_s[2, k + i] * count

        a = jnp.where(low, s_buf[pl.ds(at(0), 8), :], s_buf[pl.ds(at(1) - 4, 8), :])
        b = jnp.where(low, s_buf[pl.ds(at(2), 8), :], s_buf[pl.ds(at(3) - 4, 8), :])
        lhs = jnp.concatenate([a, b], axis=0).astype(jnp.bfloat16)
        rhs = b_buf[pl.ds(pl.multiple_of(q * 512, 512), 512), :]
        o = lax.dot_general(lhs, rhs, (((1,), (1,)), ((), ())), preferred_element_type=f32)
        top = jnp.where(low, o[0:8, 0:128], o[0:8, 128:256])
        bot = jnp.where(low, o[8:16, 256:384], o[8:16, 384:512])
        parts[pl.ds(pl.multiple_of(q * 16, 16), 16), :] = jnp.concatenate([top, bot], axis=0)
        return carry

    quads = per // 4
    for c in range(CHUNKS):
        b_copies[c].wait()
        lax.fori_loop(c * quads, (c + 1) * quads, forward, 0, unroll=24)

    srow = lax.broadcasted_iota(jnp.int32, (rec * 8, 1), 0)
    pick = jnp.where(srow // 8 == r_k, weight, 0.0)
    obs = jnp.zeros((rec * 8, 128), f32)
    for p in range(count):
        h_hi, h_lo = split(jnp.where(srow % 8 == p, pick, 0.0))
        v_hi, v_lo = split(parts[pl.ds(p, slots, stride=count), :])
        obs = obs + mm(h_hi, v_hi) + mm(h_hi, v_lo) + mm(h_lo, v_hi)
    snd[...] = (obs.reshape(rec, 8, 128) + norm[None]).reshape(n, own, 8, 128)

    pl.semaphore_wait(barrier, n - 1)

    def first(o):
        peer = lax.rem(me + o, n)
        return pltpu.make_async_remote_copy(
            src_ref=snd.at[peer],
            dst_ref=rc1.at[me],
            send_sem=send1.at[peer],
            recv_sem=recv1.at[me],
            device_id={"space": peer},
            device_id_type=MESH,
        )

    def second(o):
        peer = lax.rem(me + o, n)
        return pltpu.make_async_remote_copy(
            src_ref=gat.at[me],
            dst_ref=gat.at[me],
            send_sem=send2.at[peer],
            recv_sem=recv2.at[me],
            device_id={"space": peer},
            device_id_type=MESH,
        )

    def arrived(buf, sem, o):
        peer = lax.rem(me + o, n)
        return pltpu.make_async_remote_copy(
            src_ref=buf.at[peer],
            dst_ref=buf.at[peer],
            send_sem=sem.at[peer],
            recv_sem=sem.at[peer],
            device_id={"space": peer},
            device_id_type=MESH,
        )

    @pl.loop(1, n)
    def _(o):
        first(o).start()

    rc1[me] = snd[me]

    day = lax.broadcasted_iota(jnp.int32, (days, 1), 0)
    late = t_k - day
    grow = jnp.exp(rate * late.astype(f32)) * jnp.where(day == 0, 1.0, rest)
    grow = jnp.where(late >= 0, grow, 0.0) * weight
    for j in range(tiles):
        spread[j * days : (j + 1) * days, :] = jnp.where(j_k == j, grow, 0.0)

    @pl.loop(1, n)
    def _(o):
        arrived(rc1, recv1, o).wait_recv()

    gat[me] = jnp.sum(rc1[...], axis=0)

    @pl.loop(1, n)
    def _(o):
        second(o).start()

    @pl.loop(1, n)
    def _(o):
        first(o).wait_send()

    @pl.loop(1, n)
    def _(o):
        arrived(gat, recv2, o).wait_recv()

    total = gat[...].reshape(rec, 8, 128)
    resid = (total * noise_ref[...][:, None, :]).astype(jnp.bfloat16).astype(f32)
    for r in range(rec):
        res_buf[PAD + r * count : PAD + (r + 1) * count, :] = resid[r, :count, :]
    energy = jnp.sum(total * resid, axis=0)
    energy = energy[:count] + total[0, count:]
    curv_ref[...] = jnp.broadcast_to(jnp.sum(energy, axis=1, keepdims=True), (count, 128))

    def backward(q, carry):
        k = q * 4

        def at(i):
            return PAD + lists_s[0, k + i] * count

        outs = []
        for h in range(2):
            a = jnp.where(low, res_buf[pl.ds(at(2 * h), 8), :], 0.0)
            b = jnp.where(low, 0.0, res_buf[pl.ds(at(2 * h + 1) - 4, 8), :])
            lhs = jnp.concatenate([a, b], axis=1).astype(jnp.bfloat16)
            rhs = b_buf[pl.ds(pl.multiple_of(q * 512 + h * 256, 256), 256), :]
            outs.append(mm(lhs, rhs))
        parts[pl.ds(pl.multiple_of(q * 16, 16), 16), :] = jnp.concatenate(outs, axis=0)
        return carry

    lax.fori_loop(0, slots // 4, backward, 0, unroll=24)

    g_hi = spread[...].astype(jnp.bfloat16)
    for p in range(count):
        v_hi = parts[pl.ds(p, slots, stride=count), :].astype(jnp.bfloat16)
        image = mm(g_hi, v_hi)
        for j in range(tiles):
            here = (slice(p * days, (p + 1) * days), slice(j * 128, (j + 1) * 128))
            back = image[j * days : (j + 1) * days, :] * prior_ref[:, j * 128 : (j + 1) * 128]
            hess_ref[here] = x_buf[here] + back

    @pl.loop(1, n)
    def _(o):
        second(o).wait_send()


def shards(
    n, probes, prior_std, blocks, footprint_block_scale, block_lists, block_live, noise_inv, corr_days
):
    count, days, cells = probes.shape
    slots = blocks.shape[0]
    rec = noise_inv.shape[0] // 128
    rows = count * days
    tiles = cells // 128
    own = rec // n
    vmem = pl.BlockSpec(memory_space=pltpu.VMEM)
    smem = pl.BlockSpec(memory_space=pltpu.SMEM)
    hbm = pl.BlockSpec(memory_space=pltpu.HBM)
    dma = pltpu.SemaphoreType.DMA
    hess, curv = pl.pallas_call(
        functools.partial(kernel, n),
        out_shape=(
            jax.ShapeDtypeStruct((rows, cells), jnp.float32),
            jax.ShapeDtypeStruct((count, 128), jnp.float32),
        ),
        in_specs=[smem, smem] + [hbm] * 6,
        out_specs=(vmem, vmem),
        scratch_shapes=[
            pltpu.SMEM((3, slots), jnp.int32),
            pltpu.VMEM((3, slots), jnp.int32),
            pltpu.VMEM((slots,), jnp.float32),
            pltpu.VMEM((1, cells), jnp.float32),
            pltpu.VMEM((rec, 128), jnp.float32),
            pltpu.VMEM((rows, cells), jnp.float32),
            pltpu.VMEM((slots * 128, 128), jnp.bfloat16),
            pltpu.VMEM((tiles * rows + 2 * PAD, 128), jnp.float32),
            pltpu.VMEM((slots * count, 128), jnp.float32),
            pltpu.VMEM((rec * count + 2 * PAD, 128), jnp.float32),
            pltpu.VMEM((tiles * days, slots), jnp.float32),
            pltpu.VMEM((n, own, 8, 128), jnp.float32),
            pltpu.VMEM((n, own, 8, 128), jnp.float32),
            pltpu.VMEM((n, own, 8, 128), jnp.float32),
            dma((6,)),
            dma((CHUNKS,)),
            dma((n,)),
            dma((n,)),
            dma((n,)),
            dma((n,)),
        ],
        compiler_params=pltpu.CompilerParams(
            collective_id=0, has_side_effects=True, vmem_limit_bytes=LIMIT
        ),
    )(
        block_live,
        corr_days,
        hold(block_lists.T),
        hold(footprint_block_scale),
        hold(prior_std.reshape(1, cells)),
        hold(noise_inv.reshape(rec, 128)),
        hold(probes.reshape(rows, cells)),
        blocks.reshape(slots * 128, 128),
    )
    return hess.reshape(count, days, cells), curv[:, 0]


def solution(mesh):
    in_specs = (
        P("groups", None, "space"),
        P(("groups", "space")),
        P(("groups", "space"), None, None),
        P(("groups", "space")),
        P(("groups", "space"), None),
        P(("groups", "space")),
        P("groups"),
        P("groups"),
    )
    out_specs = (P("groups", None, "space"), P("groups"))
    return jax.shard_map(
        functools.partial(shards, mesh.shape["space"]),
        mesh=mesh,
        in_specs=in_specs,
        out_specs=out_specs,
        check_vma=False,
    )
```

```python
import functools

import jax
import jax.numpy as jnp
from jax import lax
from jax.experimental import pallas as pl
from jax.experimental.pallas import tpu as pltpu
from jax.sharding import PartitionSpec as P

MESH = pl.DeviceIdType.MESH
CHUNKS = 3
PAD = 8
LIMIT = 48 * 1024 * 1024


def hold(x):
    return pltpu.with_memory_space_constraint(x, pltpu.HBM)


def split(x):
    high = x.astype(jnp.bfloat16)
    return high, (x - high.astype(jnp.float32)).astype(jnp.bfloat16)


def mm(a, b):
    return jnp.dot(a, b, preferred_element_type=jnp.float32)


def kernel(
    n,
    live_s,
    corr_s,
    lists_hbm,
    scale_hbm,
    prior_hbm,
    noise_hbm,
    probes_hbm,
    blocks_hbm,
    hess_ref,
    curv_ref,
    lists_s,
    lists_v,
    scale_ref,
    prior_ref,
    noise_ref,
    x_buf,
    b_buf,
    s_buf,
    parts,
    res_buf,
    spread,
    snd,
    rc1,
    gat,
    in_sem,
    b_sem,
    send1,
    recv1,
    send2,
    recv2,
):
    rows, cells = x_buf.shape
    count = 4
    days = rows // count
    tiles = cells // 128
    slots = lists_v.shape[1]
    rec = noise_ref.shape[0]
    own = rec // n
    per = slots // CHUNKS
    f32 = jnp.float32
    me = lax.axis_index("space")

    x_copy = pltpu.make_async_copy(probes_hbm, x_buf, in_sem.at[0])
    x_copy.start()
    small = []
    for i, (src, dst) in enumerate(
        (
            (lists_hbm, lists_s),
            (lists_hbm, lists_v),
            (scale_hbm, scale_ref),
            (prior_hbm, prior_ref),
            (noise_hbm, noise_ref),
        )
    ):
        cp = pltpu.make_async_copy(src, dst, in_sem.at[i + 1])
        cp.start()
        small.append(cp)
    b_copies = []
    for c in range(CHUNKS):
        part = pl.ds(c * per * 128, per * 128)
        cp = pltpu.make_async_copy(blocks_hbm.at[part], b_buf.at[part], b_sem.at[c])
        cp.start()
        b_copies.append(cp)

    barrier = pltpu.get_barrier_semaphore()

    @pl.loop(1, n)
    def _(o):
        pl.semaphore_signal(
            barrier, inc=1, device_id={"space": lax.rem(me + o, n)}, device_id_type=MESH
        )

    rate = -1.0 / jnp.full((1, 1), corr_s[0], f32)
    rest = jnp.sqrt(1.0 - jnp.exp(2.0 * rate))

    row = lax.broadcasted_iota(jnp.int32, (rows, 1), 0)
    col = lax.broadcasted_iota(jnp.int32, (1, rows), 1)
    row_t, row_p = row // count, row % count
    col_p = sum((col >= days * p).astype(jnp.int32) for p in range(1, count))
    col_s = col - days * col_p
    lag = row_t - col_s
    value = jnp.exp(rate * lag.astype(f32)) * jnp.where(col_s == 0, 1.0, rest)
    factor = jnp.where((lag >= 0) & (row_p == col_p), value, 0.0)
    f_hi, f_lo = split(factor)

    for cp in small:
        cp.wait()

    r_k, j_k, t_k = lists_v[0:1, :], lists_v[1:2, :], lists_v[2:3, :]
    lane = lax.broadcasted_iota(jnp.int32, (1, slots), 1)
    weight = jnp.where(lane < live_s[0], scale_ref[...].reshape(1, slots), 0.0)

    s_buf[0:PAD, :] = jnp.zeros((PAD, 128), f32)
    s_buf[PAD + tiles * rows :, :] = jnp.zeros((PAD, 128), f32)
    res_buf[0:PAD, :] = jnp.zeros((PAD, 128), f32)
    res_buf[PAD + rec * count :, :] = jnp.zeros((PAD, 128), f32)

    x_copy.wait()
    square = jnp.zeros((rows, 128), f32)
    for j in range(0, tiles, 2):
        x = x_buf[:, j * 128 : j * 128 + 256]
        square = square + x[:, :128] * x[:, :128] + x[:, 128:] * x[:, 128:]
        x_hi, x_lo = split(x)
        moved = mm(f_hi, x_hi) + mm(f_hi, x_lo) + mm(f_lo, x_hi)
        scaled = (moved * prior_ref[:, j * 128 : j * 128 + 256]).astype(jnp.bfloat16).astype(f32)
        s_buf[PAD + j * rows : PAD + (j + 1) * rows, :] = scaled[:, :128]
        s_buf[PAD + (j + 1) * rows : PAD + (j + 2) * rows, :] = scaled[:, 128:]
    norm = jnp.sum(square.reshape(count, days, 128), axis=1)
    norm = jnp.concatenate([jnp.zeros_like(norm), norm], axis=0)

    low = lax.broadcasted_iota(jnp.int32, (8, 128), 0) < 4

    def forward(q, carry):
        k = q * 4

        def at(i):
            return PAD + lists_s[1, k + i] * rows + lists_s[2, k + i] * count

        a = jnp.where(low, s_buf[pl.ds(at(0), 8), :], s_buf[pl.ds(at(1) - 4, 8), :])
        b = jnp.where(low, s_buf[pl.ds(at(2), 8), :], s_buf[pl.ds(at(3) - 4, 8), :])
        lhs = jnp.concatenate([a, b], axis=0).astype(jnp.bfloat16)
        rhs = b_buf[pl.ds(pl.multiple_of(q * 512, 512), 512), :]
        o = lax.dot_general(lhs, rhs, (((1,), (1,)), ((), ())), preferred_element_type=f32)
        top = jnp.where(low, o[0:8, 0:128], o[0:8, 128:256])
        bot = jnp.where(low, o[8:16, 256:384], o[8:16, 384:512])
        parts[pl.ds(pl.multiple_of(q * 16, 16), 16), :] = jnp.concatenate([top, bot], axis=0)
        return carry

    quads = per // 4
    for c in range(CHUNKS):
        b_copies[c].wait()
        lax.fori_loop(c * quads, (c + 1) * quads, forward, 0, unroll=24)

    srow = lax.broadcasted_iota(jnp.int32, (rec * 8, 1), 0)
    pick = jnp.where(srow // 8 == r_k, weight, 0.0)
    obs = jnp.zeros((rec * 8, 128), f32)
    for p in range(count):
        h_hi, h_lo = split(jnp.where(srow % 8 == p, pick, 0.0))
        v_hi, v_lo = split(parts[pl.ds(p, slots, stride=count), :])
        obs = obs + mm(h_hi, v_hi) + mm(h_hi, v_lo) + mm(h_lo, v_hi)
    snd[...] = (obs.reshape(rec, 8, 128) + norm[None]).reshape(n, own, 8, 128)

    pl.semaphore_wait(barrier, n - 1)

    def first(o):
        peer = lax.rem(me + o, n)
        return pltpu.make_async_remote_copy(
            src_ref=snd.at[peer],
            dst_ref=rc1.at[me],
            send_sem=send1.at[peer],
            recv_sem=recv1.at[me],
            device_id={"space": peer},
            device_id_type=MESH,
        )

    def second(o):
        peer = lax.rem(me + o, n)
        return pltpu.make_async_remote_copy(
            src_ref=gat.at[me],
            dst_ref=gat.at[me],
            send_sem=send2.at[peer],
            recv_sem=recv2.at[me],
            device_id={"space": peer},
            device_id_type=MESH,
        )

    def arrived(buf, sem, o):
        peer = lax.rem(me + o, n)
        return pltpu.make_async_remote_copy(
            src_ref=buf.at[peer],
            dst_ref=buf.at[peer],
            send_sem=sem.at[peer],
            recv_sem=sem.at[peer],
            device_id={"space": peer},
            device_id_type=MESH,
        )

    @pl.loop(1, n)
    def _(o):
        first(o).start()

    rc1[me] = snd[me]

    day = lax.broadcasted_iota(jnp.int32, (days, 1), 0)
    late = t_k - day
    grow = jnp.exp(rate * late.astype(f32)) * jnp.where(day == 0, 1.0, rest)
    grow = jnp.where(late >= 0, grow, 0.0) * weight
    for j in range(tiles):
        spread[j * days : (j + 1) * days, :] = jnp.where(j_k == j, grow, 0.0)

    @pl.loop(1, n)
    def _(o):
        arrived(rc1, recv1, o).wait_recv()

    gat[me] = jnp.sum(rc1[...], axis=0)

    @pl.loop(1, n)
    def _(o):
        second(o).start()

    @pl.loop(1, n)
    def _(o):
        first(o).wait_send()

    @pl.loop(1, n)
    def _(o):
        arrived(gat, recv2, o).wait_recv()

    total = gat[...].reshape(rec, 8, 128)
    resid = (total * noise_ref[...][:, None, :]).astype(jnp.bfloat16).astype(f32)
    for r in range(rec):
        res_buf[PAD + r * count : PAD + (r + 1) * count, :] = resid[r, :count, :]
    energy = jnp.sum(total * resid, axis=0)
    energy = energy[:count] + total[0, count:]
    curv_ref[...] = jnp.broadcast_to(jnp.sum(energy, axis=1, keepdims=True), (count, 128))

    def backward(q, carry):
        k = q * 4

        def at(i):
            return PAD + lists_s[0, k + i] * count

        outs = []
        for h in range(2):
            a = jnp.where(low, res_buf[pl.ds(at(2 * h), 8), :], 0.0)
            b = jnp.where(low, 0.0, res_buf[pl.ds(at(2 * h + 1) - 4, 8), :])
            lhs = jnp.concatenate([a, b], axis=1).astype(jnp.bfloat16)
            rhs = b_buf[pl.ds(pl.multiple_of(q * 512 + h * 256, 256), 256), :]
            outs.append(mm(lhs, rhs))
        parts[pl.ds(pl.multiple_of(q * 16, 16), 16), :] = jnp.concatenate(outs, axis=0)
        return carry

    lax.fori_loop(0, slots // 4, backward, 0, unroll=36)

    g_hi = spread[...].astype(jnp.bfloat16)
    for p in range(count):
        v_hi = parts[pl.ds(p, slots, stride=count), :].astype(jnp.bfloat16)
        image = mm(g_hi, v_hi)
        for j in range(tiles):
            here = (slice(p * days, (p + 1) * days), slice(j * 128, (j + 1) * 128))
            back = image[j * days : (j + 1) * days, :] * prior_ref[:, j * 128 : (j + 1) * 128]
            hess_ref[here] = x_buf[here] + back

    @pl.loop(1, n)
    def _(o):
        second(o).wait_send()


def shards(
    n, probes, prior_std, blocks, footprint_block_scale, block_lists, block_live, noise_inv, corr_days
):
    count, days, cells = probes.shape
    slots = blocks.shape[0]
    rec = noise_inv.shape[0] // 128
    rows = count * days
    tiles = cells // 128
    own = rec // n
    vmem = pl.BlockSpec(memory_space=pltpu.VMEM)
    smem = pl.BlockSpec(memory_space=pltpu.SMEM)
    hbm = pl.BlockSpec(memory_space=pltpu.HBM)
    dma = pltpu.SemaphoreType.DMA
    hess, curv = pl.pallas_call(
        functools.partial(kernel, n),
        out_shape=(
            jax.ShapeDtypeStruct((rows, cells), jnp.float32),
            jax.ShapeDtypeStruct((count, 128), jnp.float32),
        ),
        in_specs=[smem, smem] + [hbm] * 6,
        out_specs=(vmem, vmem),
        scratch_shapes=[
            pltpu.SMEM((3, slots), jnp.int32),
            pltpu.VMEM((3, slots), jnp.int32),
            pltpu.VMEM((slots,), jnp.float32),
            pltpu.VMEM((1, cells), jnp.float32),
            pltpu.VMEM((rec, 128), jnp.float32),
            pltpu.VMEM((rows, cells), jnp.float32),
            pltpu.VMEM((slots * 128, 128), jnp.bfloat16),
            pltpu.VMEM((tiles * rows + 2 * PAD, 128), jnp.float32),
            pltpu.VMEM((slots * count, 128), jnp.float32),
            pltpu.VMEM((rec * count + 2 * PAD, 128), jnp.float32),
            pltpu.VMEM((tiles * days, slots), jnp.float32),
            pltpu.VMEM((n, own, 8, 128), jnp.float32),
            pltpu.VMEM((n, own, 8, 128), jnp.float32),
            pltpu.VMEM((n, own, 8, 128), jnp.float32),
            dma((6,)),
            dma((CHUNKS,)),
            dma((n,)),
            dma((n,)),
            dma((n,)),
            dma((n,)),
        ],
        compiler_params=pltpu.CompilerParams(
            collective_id=0, has_side_effects=True, vmem_limit_bytes=LIMIT
        ),
    )(
        block_live,
        corr_days,
        hold(block_lists.T),
        hold(footprint_block_scale),
        hold(prior_std.reshape(1, cells)),
        hold(noise_inv.reshape(rec, 128)),
        hold(probes.reshape(rows, cells)),
        blocks.reshape(slots * 128, 128),
    )
    return hess.reshape(count, days, cells), curv[:, 0]


def solution(mesh):
    in_specs = (
        P("groups", None, "space"),
        P(("groups", "space")),
        P(("groups", "space"), None, None),
        P(("groups", "space")),
        P(("groups", "space"), None),
        P(("groups", "space")),
        P("groups"),
        P("groups"),
    )
    out_specs = (P("groups", None, "space"), P("groups"))
    return jax.shard_map(
        functools.partial(shards, mesh.shape["space"]),
        mesh=mesh,
        in_specs=in_specs,
        out_specs=out_specs,
        check_vma=False,
    )
```
